32 devices in a mesh: ctx: 8 (over z, y), head: 4 (over x, core).
Axes of the slice: x: 2, y: 2, z: 4, core: 2. Of those that a mesh axis runs over, the one named last changes fastest.
Arguments:
- queries: bfloat16 [3072, 8, 128], P('ctx', 'head'), may hold values from -6 to 6
- key_rows: bfloat16 [3072, 128], P('ctx'), may hold values from -6 to 6
- value_rows: bfloat16 [3072, 128], P('ctx'), may hold values from -6 to 6
- grad_out: bfloat16 [3072, 8, 128], P('ctx', 'head'), may hold values from -6 to 6
- doc_lengths: int32 [64], replicated, may hold values from 1 to 2304, as said below
- block_pattern: int32 [24, 24], P('ctx'), may hold values from 0 to 1, as said below
Outputs:
- attn_out: bfloat16 [3072, 8, 128], P('ctx', 'head')
- grad_queries: bfloat16 [3072, 8, 128], P('ctx', 'head')
- grad_keys: bfloat16 [3072, 128], P('ctx')
- grad_values: bfloat16 [3072, 128], P('ctx')
The draws below stay inside these ranges and needn't reach their ends.
Inputs may be any that keep to these rules, and one draw needn't show every extreme that they name: block_pattern[i, j] is 0 unless i // 3 - j // 3 is 0 or a positive power of two; it is 1 where i == j. `doc_lengths`: the lengths sum to 3072; the first document has exactly 2304 positions.
All inputs are finite; a program needn't handle non-finite values.
Results may differ from the reference program's by a relative error of at most 0.017.
Values may be sent and summed in bfloat16 or wider, within the bound.
A program may use at most 64 MiB of HBM per device.

```python
import math
import jax
import jax.numpy as jnp
from jax import lax

HEADS = 8
DH = 128
TOK_DEV = 384
BLOCK = 128
DOCS = 64
TOKENS = 3072
BLK_DEV = 3
NBLK = 24
LEVELS = 3
N_CTX = 8


def draw_queries(key, part):
    noise = jnp.clip(jax.random.normal(jax.random.fold_in(key, 1), (TOKENS, HEADS, DH), jnp.float32), -6.0, 6.0)
    return noise.astype(jnp.bfloat16)


def draw_key_rows(key, part):
    noise = jnp.clip(jax.random.normal(jax.random.fold_in(key, 2), (TOKENS, DH), jnp.float32), -6.0, 6.0)
    return noise.astype(jnp.bfloat16)


def draw_doc_lengths(key, part):
    rest_total = TOKENS - 3 * TOKENS // 4
    order = jax.random.permutation(jax.random.fold_in(key, 5), rest_total - 1)
    cuts = jnp.sort(order[:DOCS - 2] + 1).astype(jnp.int32)
    edges = jnp.concatenate([jnp.zeros((1,), jnp.int32), cuts, jnp.full((1,), rest_total, jnp.int32)])
    rest_lengths = (edges[1:] - edges[:-1]).astype(jnp.int32)
    return jnp.concatenate([jnp.full((1,), 3 * TOKENS // 4, jnp.int32), rest_lengths]).astype(jnp.int32)


def draw_block_pattern(key, part):
    block_ids = jnp.arange(NBLK, dtype=jnp.int32)
    shard_gap = block_ids[:, None] // BLK_DEV - block_ids[None, :] // BLK_DEV
    allowed = (shard_gap >= 0) & (jnp.bitwise_and(shard_gap, shard_gap - 1) == 0)
    kept = jax.random.randint(jax.random.fold_in(key, 3), (NBLK, NBLK), 0, 4) != 0
    diagonal = block_ids[:, None] == block_ids[None, :]
    return jnp.where(allowed & (kept | diagonal), 1, 0).astype(jnp.int32)


def level_of(rng, shape, split, least, high):
    gain, own = 1.0, jax.random.fold_in(rng, 6)
    for dim, shards_of in split:
        heights = jnp.exp(jax.random.uniform(jax.random.fold_in(own, dim), (shards_of,), jnp.float32, least / len(split), high / len(split)))
        gain = gain * jnp.repeat(heights, shape[dim] // shards_of).reshape([-1 if axis == dim else 1 for axis in range(len(shape))])
    return gain


def gaussian(rng, extent, width, bound, split=(), kind=jnp.bfloat16):
    level = level_of(rng, extent, split, -0.22, 0.18) if split else 1.0
    result = jax.random.normal(rng, extent, jnp.float32) * width * level
    return jnp.minimum(jnp.maximum(result, -bound), bound).astype(kind)


def setup_inputs(seed: int = 0) -> dict:
    keys = jax.random.split(jax.random.key(seed), 7)
    queries = draw_queries(jax.random.fold_in(keys[6], 71), 0)
    key_rows = draw_key_rows(jax.random.fold_in(keys[6], 71), 0)
    value_rows = gaussian(keys[2], (TOKENS, DH), 1.0, 6.0, ((0, 8),))
    grad_out = gaussian(keys[3], (TOKENS, HEADS, DH), 1.0, 6.0, ((0, 8), (1, 4)))
    doc_lengths = draw_doc_lengths(jax.random.fold_in(keys[6], 71), 0)
    block_pattern = draw_block_pattern(jax.random.fold_in(keys[6], 71), 0)
    return {"queries": queries, "key_rows": key_rows, "value_rows": value_rows, "grad_out": grad_out, "doc_lengths": doc_lengths, "block_pattern": block_pattern}


NEG_FILL = -1e+30

def doc_index(doc_lengths, positions):
    doc_ends = jnp.cumsum(doc_lengths, dtype=jnp.int32)
    return lax.optimization_barrier(jnp.sum((doc_ends[None, :] <= positions[:, None]).astype(jnp.int32), axis=1))

def pair_mask(pattern_rows, query_shard, key_shard, doc_lengths):
    offsets = jnp.arange(TOK_DEV, dtype=jnp.int32)
    query_pos = query_shard * TOK_DEV + offsets
    key_pos = key_shard * TOK_DEV + offsets
    blocks_live = lax.dynamic_slice_in_dim(pattern_rows, (key_shard * BLK_DEV).astype(jnp.int32), BLK_DEV, 1)
    blocks_live = jnp.repeat(jnp.repeat(blocks_live, BLOCK, axis=0), BLOCK, axis=1)
    same_doc = doc_index(doc_lengths, query_pos)[:, None] == doc_index(doc_lengths, key_pos)[None, :]
    return (blocks_live == 1) & same_doc & (key_pos[None, :] <= query_pos[:, None])

def to_low(array):
    return lax.optimization_barrier(array.astype(jnp.bfloat16)).astype(jnp.float32)

def reference(queries, key_rows, value_rows, grad_out, doc_lengths, block_pattern):
    score_scale = 1.0 / math.sqrt(DH)

    def shard_step(carried, query_shard):
        keys_grad, values_grad = carried
        row_start = (query_shard * TOK_DEV).astype(jnp.int32)
        q_rows = lax.dynamic_slice_in_dim(queries, row_start, TOK_DEV, 0).astype(jnp.float32)
        out_grad = lax.dynamic_slice_in_dim(grad_out, row_start, TOK_DEV, 0).astype(jnp.float32)
        pattern_rows = lax.dynamic_slice_in_dim(block_pattern, (query_shard * BLK_DEV).astype(jnp.int32), BLK_DEV, 0)
        raw_partners = [query_shard] + [query_shard - jnp.int32(1 << bit_index) for bit_index in range(LEVELS)]
        partners = [jnp.maximum(item, 0).astype(jnp.int32) for item in raw_partners]
        valid_list = [item >= 0 for item in raw_partners]
        key_list = []
        value_list = []
        mask_list = []
        score_list = []
        for partner, valid in zip(partners, valid_list):
            key_start = (partner * TOK_DEV).astype(jnp.int32)
            key_here = lax.dynamic_slice_in_dim(key_rows, key_start, TOK_DEV, 0).astype(jnp.float32)
            value_here = lax.dynamic_slice_in_dim(value_rows, key_start, TOK_DEV, 0).astype(jnp.float32)
            live_mask = pair_mask(pattern_rows, query_shard, partner, doc_lengths) & valid
            raw_scores = jnp.einsum('thd,ud->htu', q_rows, key_here) * score_scale
            key_list.append(key_here)
            value_list.append(value_here)
            mask_list.append(live_mask)
            score_list.append(jnp.where(live_mask[None], raw_scores, NEG_FILL))
        row_max = score_list[0].max(axis=-1)
        for scores in score_list[1:]:
            row_max = jnp.maximum(row_max, scores.max(axis=-1))
        row_total = jnp.zeros_like(row_max)
        for scores, live_mask in zip(score_list, mask_list):
            row_total = row_total + lax.optimization_barrier(jnp.sum(jnp.where(live_mask[None], jnp.exp(scores - row_max[..., None]), 0.0), axis=-1))
        prob_list = []
        out_acc = jnp.zeros((TOK_DEV, HEADS, DH), jnp.float32)
        for scores, live_mask, value_here in zip(score_list, mask_list, value_list):
            probs = jnp.where(live_mask[None], jnp.exp(scores - row_max[..., None]) / row_total[..., None], 0.0)
            prob_list.append(probs)
            out_acc = out_acc + jnp.einsum('htu,ud->thd', to_low(probs), value_here)
        attn_rows = out_acc.astype(jnp.bfloat16)
        out_dot = lax.optimization_barrier(jnp.sum(out_grad * attn_rows.astype(jnp.float32), axis=-1)).T
        query_grad = jnp.zeros((TOK_DEV, HEADS, DH), jnp.float32)
        for partner, probs, key_here, value_here in zip(partners, prob_list, key_list, value_list):
            grad_prob = jnp.einsum('thd,ud->htu', out_grad, value_here)
            grad_score = to_low(probs * (grad_prob - out_dot[..., None]) * score_scale)
            query_grad = query_grad + jnp.einsum('htu,ud->thd', grad_score, key_here)
            part_key = jnp.einsum('htu,thd->ud', grad_score, q_rows)
            part_value = jnp.einsum('htu,thd->ud', to_low(probs), out_grad)
            key_start = (partner * TOK_DEV).astype(jnp.int32)
            keys_grad = lax.dynamic_update_slice_in_dim(keys_grad, lax.dynamic_slice_in_dim(keys_grad, key_start, TOK_DEV, 0) + part_key, key_start, 0)
            values_grad = lax.dynamic_update_slice_in_dim(values_grad, lax.dynamic_slice_in_dim(values_grad, key_start, TOK_DEV, 0) + part_value, key_start, 0)
        return ((keys_grad, values_grad), (attn_rows, query_grad.astype(jnp.bfloat16)))
    start_grads = (jnp.zeros((TOKENS, DH), jnp.float32), jnp.zeros((TOKENS, DH), jnp.float32))
    (keys_grad, values_grad), (attn_all, query_all) = lax.scan(shard_step, start_grads, jnp.arange(N_CTX, dtype=jnp.int32))
    attn_out = attn_all.reshape(TOKENS, HEADS, DH)
    grad_queries = query_all.reshape(TOKENS, HEADS, DH)
    return (attn_out, grad_queries, keys_grad.astype(jnp.bfloat16), values_grad.astype(jnp.bfloat16))
```

```python
import functools
import math

import jax
import jax.numpy as jnp
from jax import lax
from jax.experimental import pallas as pl
from jax.experimental.pallas import tpu as pltpu
from jax.sharding import PartitionSpec as P

NEG_FILL = -1e30
FAR = 1e9
MESH = pl.DeviceIdType.MESH
F32 = jnp.float32
LOW = jnp.bfloat16


def dot(a, b, dim_a, dim_b):
    return lax.dot_general(
        a, b, (((dim_a,), (dim_b,)), ((), ())), preferred_element_type=F32
    )


def remote(src, dst, sent, landed, ctx, head):
    return pltpu.make_async_remote_copy(
        src_ref=src,
        dst_ref=dst,
        send_sem=sent,
        recv_sem=landed,
        device_id=(ctx, head),
        device_id_type=MESH,
    )


def kernel(
    ctx_width, head_width, group, pattern, lengths, q_in, k_in, v_in, g_in,
    o_out, dq_out, dk_out, dv_out,
    kv, q, g, e, f, dp, top, tot, acc, mean, low_buf, dq_buf,
    keep, swap_out, swap_in, flow_out, flow_in, total, final,
    load_sem, store_sem, kv_sent, kv_landed, pair_sent, pair_landed,
    swap_sent, swap_landed, flow_sent, flow_landed, fin_sent, fin_landed,
):
    tok_rows, dim = k_in.shape
    rows = q_in.shape[0]
    block_count = pattern.shape[0]
    block = tok_rows // block_count
    block_q = block * group
    sections = kv.shape[0]
    parts = head_width // 2
    part_rows = tok_rows // parts
    scale = 1.0 / math.sqrt(dim)
    first_doc = 3 * ctx_width // 4
    c = lax.axis_index("ctx")
    h = lax.axis_index("head")
    kind = lax.rem(h, 2)
    x = lax.div(h, 2)
    sibling = h + 1 - 2 * kind
    gaps = [0] + [1 << bit for bit in range(sections - 1)]

    def sends(s):
        d = gaps[s]
        crosses = jnp.logical_and(c < first_doc, c + d >= first_doc)
        return jnp.logical_and(c + d < ctx_width, jnp.logical_not(crosses))

    def takes(s):
        d = gaps[s]
        crosses = jnp.logical_and(c - d < first_doc, c >= first_doc)
        return jnp.logical_and(c - d >= 0, jnp.logical_not(crosses))

    loads = [
        pltpu.make_async_copy(k_in, kv.at[0, 0], load_sem.at[0]),
        pltpu.make_async_copy(v_in, kv.at[0, 1], load_sem.at[1]),
        pltpu.make_async_copy(q_in, q, load_sem.at[2]),
        pltpu.make_async_copy(g_in, g, load_sem.at[3]),
    ]
    for load in loads:
        load.start()

    barrier = pltpu.get_barrier_semaphore()
    expected = jnp.int32(head_width - 1)
    for o in range(1, head_width):
        pl.semaphore_signal(
            barrier, inc=1, device_id=(c, lax.rem(h + o, head_width)), device_id_type=MESH
        )
    for s in range(1, sections):
        for sign, active in ((1, sends(s)), (-1, takes(s))):
            expected = expected + jnp.where(active, parts, 0)

            @pl.when(active)
            def _():
                for xp in range(parts):
                    pl.semaphore_signal(
                        barrier,
                        inc=1,
                        device_id=(c + sign * gaps[s], 2 * xp + kind),
                        device_id_type=MESH,
                    )
    pl.semaphore_wait(barrier, expected)

    def kv_copy(s):
        return remote(
            kv.at[0, kind], kv.at[s, kind], kv_sent.at[s], kv_landed.at[s], c + gaps[s], h
        )

    def pair_copy(s, which):
        return remote(
            kv.at[s, which], kv.at[s, which], pair_sent.at[s], pair_landed.at[s], c, sibling
        )

    loads[0].wait()
    loads[1].wait()
    for s in range(1, sections):
        pl.when(sends(s))(lambda: kv_copy(s).start())
    loads[2].wait()
    loads[3].wait()

    doc_count = lengths.shape[1]
    len_row = lengths[...].astype(F32)
    row_id = lax.broadcasted_iota(jnp.int32, (doc_count, doc_count), 0)
    col_id = lax.broadcasted_iota(jnp.int32, (doc_count, doc_count), 1)
    len_col = jnp.sum(jnp.where(row_id == col_id, len_row, 0.0), axis=1, keepdims=True)
    ends = jnp.sum(jnp.where(row_id <= col_id, len_col, 0.0), axis=0, keepdims=True)
    shift = group.bit_length() - 1
    local_pos = lax.shift_right_logical(
        lax.broadcasted_iota(jnp.int32, (rows, doc_count), 0), shift
    )
    pos = (local_pos + c * tok_rows).astype(F32)
    begin = jnp.max(jnp.where(ends <= pos, ends, 0.0), axis=1, keepdims=True)
    lane = lax.broadcasted_iota(jnp.int32, (block_q, block), 1).astype(F32)
    in_block = lax.shift_right_logical(
        lax.broadcasted_iota(jnp.int32, (block_q, block), 0), shift
    ).astype(F32)
    log_scale = scale * math.log2(math.e)

    def forward(s):
        p = c - gaps[s]
        keys = kv[s, 0]
        values = kv[s, 1]
        with_ones = jnp.concatenate([values, jnp.ones((tok_rows, dim), LOW)], axis=1)
        for i in range(block_count):
            at = pl.ds(i * block_q, block_q)
            raw = dot(q[at], keys, 1, 1)
            tiles = []
            for j in range(block_count):
                tile = raw[:, j * block : (j + 1) * block] * log_scale
                if s == 0 and j > i:
                    tiles.append(jnp.full_like(tile, NEG_FILL))
                    continue
                base = (p * tok_rows + j * block).astype(F32)
                least = begin[i * block_q : (i + 1) * block_q] - base
                least = jnp.where(pattern[i, p * block_count + j] == 1, least, FAR)
                live = lane >= least
                if s == 0 and j == i:
                    live = jnp.logical_and(live, lane <= in_block)
                tiles.append(jnp.where(live, tile, NEG_FILL))
            scores = jnp.concatenate(tiles, axis=1)
            high = jnp.max(scores, axis=1, keepdims=True)
            ex = jnp.exp2(scores - high).astype(LOW)
            e[s, at] = ex
            top[s, at] = jnp.broadcast_to(high, (block_q, dim))
            both = dot(ex, with_ones, 1, 0)
            acc[s, at] = both[:, :dim]
            tot[s, at] = both[:, dim:]
            dp[s, at] = dot(g[at], values, 1, 1)

    forward(0)
    for s in range(1, sections):

        @pl.when(takes(s))
        def _():
            kv_copy(s).wait_recv()
            pair_copy(s, kind).start()

    for s in range(1, sections):
        active = takes(s)

        @pl.when(active)
        def _():
            pair_copy(s, 1 - kind).wait_recv()
            forward(s)

        @pl.when(jnp.logical_not(active))
        def _():
            top[s] = jnp.full((rows, dim), NEG_FILL, F32)
            tot[s] = jnp.zeros((rows, dim), F32)
            acc[s] = jnp.zeros((rows, dim), F32)

    for i in range(block_count):
        at = pl.ds(i * block_q, block_q)
        high = top[0, at]
        for s in range(1, sections):
            high = jnp.maximum(high, top[s, at])
        row_total = jnp.zeros((block_q, dim), F32)
        out = jnp.zeros((block_q, dim), F32)
        weights = []
        for s in range(sections):
            w = jnp.exp2(top[s, at] - high)
            weights.append(w)
            row_total = row_total + w * tot[s, at]
            out = out + w * acc[s, at]
        inverse = 1.0 / row_total
        low = (out * inverse).astype(LOW)
        low_buf[at] = low
        for s in range(sections):
            top[s, at] = weights[s] * inverse
        dots = jnp.sum(g[at].astype(F32) * low.astype(F32), axis=1, keepdims=True)
        mean[at] = jnp.broadcast_to(dots, (block_q, dim))
    o_store = pltpu.make_async_copy(low_buf, o_out, store_sem.at[0])
    o_store.start()

    def swap_copy(s):
        return remote(
            swap_out.at[s], swap_in.at[s], swap_sent.at[s], swap_landed.at[s], c, sibling
        )

    def backward(s):
        for i in range(block_count):
            at = pl.ds(i * block_q, block_q)
            centre = mean[at]
            for j in range(block_count):
                lanes = pl.ds(j * block, block)
                f[s, at, lanes] = (
                    e[s, at, lanes].astype(F32) * (dp[s, at, lanes] - centre)
                ).astype(LOW)
        ratio = top[s]
        q_scaled = (q[...].astype(F32) * (ratio * scale)).astype(LOW)
        g_scaled = (g[...].astype(F32) * ratio).astype(LOW)
        dk = dot(f[s], q_scaled, 0, 0)
        dv = dot(e[s], g_scaled, 0, 0)
        keep[s] = jnp.where(kind == 0, dk, dv)
        swap_out[s] = jnp.where(kind == 0, dv, dk).astype(LOW)
        swap_copy(s).start()

    for s in range(sections - 1, 0, -1):
        pl.when(takes(s))(lambda: backward(s))
    backward(0)

    def flow_copy(s, xp):
        return remote(
            flow_out.at[s, pl.ds(pl.multiple_of(xp * part_rows, 16), part_rows)],
            flow_in.at[s, x],
            flow_sent.at[s, xp],
            flow_landed.at[s, x],
            c - gaps[s],
            2 * xp + kind,
        )

    def flow_wait(s, xs):
        remote(
            flow_out.at[s, pl.ds(0, part_rows)],
            flow_in.at[s, xs],
            flow_sent.at[s, 0],
            flow_landed.at[s, xs],
            c,
            sibling,
        ).wait_recv()

    others = [lax.rem(x + o, parts) for o in range(1, parts)]

    def pass_on(s):
        swap_copy(s).wait_recv()
        joined = keep[s] + swap_in[s].astype(F32)
        if s == 0:
            keep[0] = joined
        flow_out[s] = joined.astype(LOW)
        for xp in range(parts) if s else others:
            flow_copy(s, xp).start()

    for s in range(sections - 1, 0, -1):
        pl.when(takes(s))(lambda: pass_on(s))
    pass_on(0)

    dq_buf[...] = dot(f[0], kv[0, 0], 1, 0) * top[0]
    for s in range(1, sections):

        @pl.when(takes(s))
        def _():
            dq_buf[...] += dot(f[s], kv[s, 0], 1, 0) * top[s]

    o_store.wait()
    low_buf[...] = (dq_buf[...] * scale).astype(LOW)
    dq_store = pltpu.make_async_copy(low_buf, dq_out, store_sem.at[1])
    dq_store.start()

    mine = pl.ds(pl.multiple_of(x * part_rows, 16), part_rows)
    total[...] = keep[0, mine]
    for xs in others:
        flow_wait(0, xs)
        total[...] += flow_in[0, xs].astype(F32)
    for s in range(1, sections):

        @pl.when(sends(s))
        def _():
            for xs in range(parts):
                flow_wait(s, xs)
                total[...] += flow_in[s, xs].astype(F32)

    final[...] = total[...].astype(LOW)

    def fin_copy(out, o):
        return remote(
            final, out.at[mine], fin_sent.at[o], fin_landed.at[o], c, lax.rem(h + o, head_width)
        )

    for which, out in ((0, dk_out), (1, dv_out)):

        @pl.when(kind == which)
        def _():
            for o in range(1, head_width):
                fin_copy(out, o).start()
            own = pltpu.make_async_copy(final, out.at[mine], store_sem.at[2])
            own.start()
            own.wait()

    for o in range(1, head_width):
        source = lax.rem(h + head_width - o, head_width)
        there = pl.ds(pl.multiple_of(lax.div(source, 2) * part_rows, 16), part_rows)
        for which, out in ((0, dk_out), (1, dv_out)):

            @pl.when(lax.rem(source, 2) == which)
            def _():
                remote(
                    final, out.at[there], fin_sent.at[o], fin_landed.at[o], c, source
                ).wait_recv()

    for s in range(1, sections):
        pl.when(sends(s))(lambda: kv_copy(s).wait_send())

        @pl.when(takes(s))
        def _():
            pair_copy(s, kind).wait_send()
            swap_copy(s).wait_send()
            for xp in range(parts):
                flow_copy(s, xp).wait_send()

    swap_copy(0).wait_send()
    for xp in others:
        flow_copy(0, xp).wait_send()
    for o in range(1, head_width):
        fin_copy(dk_out, o).wait_send()
    dq_store.wait()


def local(ctx_width, head_width, queries, key_rows, value_rows, grad_out, doc_lengths, block_pattern):
    tok_rows, group, dim = queries.shape
    rows = tok_rows * group
    sections = ctx_width.bit_length()
    parts = head_width // 2
    part_rows = tok_rows // parts
    anywhere = pl.BlockSpec(memory_space=pl.ANY)
    dma = pltpu.SemaphoreType.DMA
    outs = pl.pallas_call(
        functools.partial(kernel, ctx_width, head_width, group),
        out_shape=(
            jax.ShapeDtypeStruct((rows, dim), LOW),
            jax.ShapeDtypeStruct((rows, dim), LOW),
            jax.ShapeDtypeStruct((tok_rows, dim), LOW),
            jax.ShapeDtypeStruct((tok_rows, dim), LOW),
        ),
        in_specs=[
            pl.BlockSpec(memory_space=pltpu.SMEM),
            pl.BlockSpec(memory_space=pltpu.VMEM),
        ]
        + [anywhere] * 4,
        out_specs=(anywhere,) * 4,
        scratch_shapes=[
            pltpu.VMEM((sections, 2, tok_rows, dim), LOW),
            pltpu.VMEM((rows, dim), LOW),
            pltpu.VMEM((rows, dim), LOW),
            pltpu.VMEM((sections, rows, tok_rows), LOW),
            pltpu.VMEM((sections, rows, tok_rows), LOW),
            pltpu.VMEM((sections, rows, tok_rows), F32),
            pltpu.VMEM((sections, rows, dim), F32),
            pltpu.VMEM((sections, rows, dim), F32),
            pltpu.VMEM((sections, rows, dim), F32),
            pltpu.VMEM((rows, dim), F32),
            pltpu.VMEM((rows, dim), LOW),
            pltpu.VMEM((rows, dim), F32),
            pltpu.VMEM((sections, tok_rows, dim), F32),
            pltpu.VMEM((sections, tok_rows, dim), LOW),
            pltpu.VMEM((sections, tok_rows, dim), LOW),
            pltpu.VMEM((sections, tok_rows, dim), LOW),
            pltpu.VMEM((sections, parts, part_rows, dim), LOW),
            pltpu.VMEM((part_rows, dim), F32),
            pltpu.VMEM((part_rows, dim), LOW),
            dma((4,)),
            dma((3,)),
            dma((sections,)),
            dma((sections,)),
            dma((sections,)),
            dma((sections,)),
            dma((sections,)),
            dma((sections,)),
            dma((sections, parts)),
            dma((sections, parts)),
            dma((head_width,)),
            dma((head_width,)),
        ],
        compiler_params=pltpu.CompilerParams(
            collective_id=0,
            has_side_effects=True,
            vmem_limit_bytes=(12 + 5 * sections) * 1024 * 1024,
        ),
    )(
        block_pattern,
        doc_lengths.reshape(1, -1),
        queries.reshape(rows, dim),
        key_rows,
        value_rows,
        grad_out.reshape(rows, dim),
    )
    attn_out, grad_queries, grad_keys, grad_values = outs
    shape = (tok_rows, group, dim)
    return (attn_out.reshape(shape), grad_queries.reshape(shape), grad_keys, grad_values)


def solution(mesh):
    placed = (
        P("ctx", "head", None),
        P("ctx", None),
        P("ctx", None),
        P("ctx", "head", None),
        P(),
        P("ctx", None),
    )
    return jax.shard_map(
        functools.partial(local, mesh.shape["ctx"], mesh.shape["head"]),
        mesh=mesh,
        in_specs=placed,
        out_specs=(P("ctx", "head", None), P("ctx", "head", None), P("ctx", None), P("ctx", None)),
        check_vma=False,
    )
```

```python
import functools
import math

import jax
import jax.numpy as jnp
from jax import lax
from jax.experimental import pallas as pl
from jax.experimental.pallas import tpu as pltpu
from jax.sharding import PartitionSpec as P

NEG_FILL = -1e30
FAR = 1e9
MESH = pl.DeviceIdType.MESH
F32 = jnp.float32
LOW = jnp.bfloat16


def dot(a, b, dim_a, dim_b):
    return lax.dot_general(
        a, b, (((dim_a,), (dim_b,)), ((), ())), preferred_element_type=F32
    )


def remote(src, dst, sent, landed, ctx, head):
    return pltpu.make_async_remote_copy(
        src_ref=src,
        dst_ref=dst,
        send_sem=sent,
        recv_sem=landed,
        device_id=(ctx, head),
        device_id_type=MESH,
    )


def kernel(
    ctx_width, head_width, group, pattern_in, lengths_in, q_in, k_in, v_in, g_in,
    o_out, dq_out, dk_out, dv_out,
    kv, q, g, e, f, dp, top, tot, acc, mean, low_buf, dq_buf,
    keep, swap_out, swap_in, flow_out, flow_in, total, final, pattern, lengths,
    load_sem, store_sem, kv_sent, kv_landed, pair_sent, pair_landed,
    swap_sent, swap_landed, flow_sent, flow_landed, fin_sent, fin_landed,
):
    tok_rows, dim = k_in.shape
    rows = q_in.shape[0]
    block_count = pattern.shape[0]
    block = tok_rows // block_count
    block_q = block * group
    sections = kv.shape[0]
    parts = head_width // 2
    part_rows = tok_rows // parts
    scale = 1.0 / math.sqrt(dim)
    first_doc = 3 * ctx_width // 4
    c = lax.axis_index("ctx")
    h = lax.axis_index("head")
    kind = lax.rem(h, 2)
    x = lax.div(h, 2)
    sibling = h + 1 - 2 * kind
    gaps = [0] + [1 << bit for bit in range(sections - 1)]

    def sends(s):
        d = gaps[s]
        crosses = jnp.logical_and(c < first_doc, c + d >= first_doc)
        return jnp.logical_and(c + d < ctx_width, jnp.logical_not(crosses))

    def takes(s):
        d = gaps[s]
        crosses = jnp.logical_and(c - d < first_doc, c >= first_doc)
        return jnp.logical_and(c - d >= 0, jnp.logical_not(crosses))

    loads = [
        pltpu.make_async_copy(k_in, kv.at[0, 0], load_sem.at[0]),
        pltpu.make_async_copy(v_in, kv.at[0, 1], load_sem.at[1]),
        pltpu.make_async_copy(q_in, q, load_sem.at[2]),
        pltpu.make_async_copy(g_in, g, load_sem.at[3]),
        pltpu.make_async_copy(pattern_in, pattern, load_sem.at[4]),
        pltpu.make_async_copy(lengths_in, lengths, load_sem.at[5]),
    ]
    for load in loads:
        load.start()

    barrier = pltpu.get_barrier_semaphore()
    expected = jnp.int32(head_width - 1)
    for o in range(1, head_width):
        pl.semaphore_signal(
            barrier, inc=1, device_id=(c, lax.rem(h + o, head_width)), device_id_type=MESH
        )
    for s in range(1, sections):
        for sign, active in ((1, sends(s)), (-1, takes(s))):
            expected = expected + jnp.where(active, parts, 0)

            @pl.when(active)
            def _():
                for xp in range(parts):
                    pl.semaphore_signal(
                        barrier,
                        inc=1,
                        device_id=(c + sign * gaps[s], 2 * xp + kind),
                        device_id_type=MESH,
                    )
    pl.semaphore_wait(barrier, expected)

    def kv_copy(s):
        return remote(
            kv.at[0, kind], kv.at[s, kind], kv_sent.at[s], kv_landed.at[s], c + gaps[s], h
        )

    def pair_copy(s, which):
        return remote(
            kv.at[s, which], kv.at[s, which], pair_sent.at[s], pair_landed.at[s], c, sibling
        )

    loads[0].wait()
    loads[1].wait()
    for s in range(1, sections):
        pl.when(sends(s))(lambda: kv_copy(s).start())
    for load in loads[2:]:
        load.wait()

    doc_count = lengths.shape[1]
    len_row = lengths[...].astype(F32)
    row_id = lax.broadcasted_iota(jnp.int32, (doc_count, doc_count), 0)
    col_id = lax.broadcasted_iota(jnp.int32, (doc_count, doc_count), 1)
    len_col = jnp.sum(jnp.where(row_id == col_id, len_row, 0.0), axis=1, keepdims=True)
    ends = jnp.sum(jnp.where(row_id <= col_id, len_col, 0.0), axis=0, keepdims=True)
    shift = group.bit_length() - 1
    local_pos = lax.shift_right_logical(
        lax.broadcasted_iota(jnp.int32, (rows, doc_count), 0), shift
    )
    pos = (local_pos + c * tok_rows).astype(F32)
    begin = jnp.max(jnp.where(ends <= pos, ends, 0.0), axis=1, keepdims=True)
    lane = lax.broadcasted_iota(jnp.int32, (block_q, block), 1).astype(F32)
    in_block = lax.shift_right_logical(
        lax.broadcasted_iota(jnp.int32, (block_q, block), 0), shift
    ).astype(F32)
    log_scale = scale * math.log2(math.e)

    def forward(s):
        p = c - gaps[s]
        keys = kv[s, 0]
        values = kv[s, 1]
        with_ones = jnp.concatenate([values, jnp.ones((tok_rows, dim), LOW)], axis=1)
        for i in range(block_count):
            at = pl.ds(i * block_q, block_q)
            raw = dot(q[at], keys, 1, 1)
            tiles = []
            for j in range(block_count):
                tile = raw[:, j * block : (j + 1) * block] * log_scale
                if s == 0 and j > i:
                    tiles.append(jnp.full_like(tile, NEG_FILL))
                    continue
                base = (p * tok_rows + j * block).astype(F32)
                least = begin[i * block_q : (i + 1) * block_q] - base
                least = jnp.where(pattern[i, p * block_count + j] == 1, least, FAR)
                live = lane >= least
                if s == 0 and j == i:
                    live = jnp.logical_and(live, lane <= in_block)
                tiles.append(jnp.where(live, tile, NEG_FILL))
            scores = jnp.concatenate(tiles, axis=1)
            high = jnp.max(scores, axis=1, keepdims=True)
            ex = jnp.exp2(scores - high).astype(LOW)
            e[s, at] = ex
            top[s, at] = jnp.broadcast_to(high, (block_q, dim))
            both = dot(ex, with_ones, 1, 0)
            acc[s, at] = both[:, :dim]
            tot[s, at] = both[:, dim:]
            dp[s, at] = dot(g[at], values, 1, 1)

    forward(0)
    for s in range(1, sections):

        @pl.when(takes(s))
        def _():
            kv_copy(s).wait_recv()
            pair_copy(s, kind).start()

    for s in range(1, sections):
        active = takes(s)

        @pl.when(active)
        def _():
            pair_copy(s, 1 - kind).wait_recv()
            forward(s)

        @pl.when(jnp.logical_not(active))
        def _():
            top[s] = jnp.full((rows, dim), NEG_FILL, F32)
            tot[s] = jnp.zeros((rows, dim), F32)
            acc[s] = jnp.zeros((rows, dim), F32)

    for i in range(block_count):
        at = pl.ds(i * block_q, block_q)
        high = top[0, at]
        for s in range(1, sections):
            high = jnp.maximum(high, top[s, at])
        row_total = jnp.zeros((block_q, dim), F32)
        out = jnp.zeros((block_q, dim), F32)
        weights = []
        for s in range(sections):
            w = jnp.exp2(top[s, at] - high)
            weights.append(w)
            row_total = row_total + w * tot[s, at]
            out = out + w * acc[s, at]
        inverse = 1.0 / row_total
        low = (out * inverse).astype(LOW)
        low_buf[at] = low
        for s in range(sections):
            top[s, at] = weights[s] * inverse
        dots = jnp.sum(g[at].astype(F32) * low.astype(F32), axis=1, keepdims=True)
        mean[at] = jnp.broadcast_to(dots, (block_q, dim))
    o_store = pltpu.make_async_copy(low_buf, o_out, store_sem.at[0])
    o_store.start()

    def swap_copy(s):
        return remote(
            swap_out.at[s], swap_in.at[s], swap_sent.at[s], swap_landed.at[s], c, sibling
        )

    def backward(s):
        for i in range(block_count):
            at = pl.ds(i * block_q, block_q)
            centre = mean[at]
            for j in range(block_count):
                lanes = pl.ds(j * block, block)
                f[s, at, lanes] = (
                    e[s, at, lanes].astype(F32) * (dp[s, at, lanes] - centre)
                ).astype(LOW)
        ratio = top[s]
        q_scaled = (q[...].astype(F32) * (ratio * scale)).astype(LOW)
        g_scaled = (g[...].astype(F32) * ratio).astype(LOW)
        dk = dot(f[s], q_scaled, 0, 0)
        dv = dot(e[s], g_scaled, 0, 0)
        keep[s] = jnp.where(kind == 0, dk, dv)
        swap_out[s] = jnp.where(kind == 0, dv, dk).astype(LOW)
        swap_copy(s).start()

    def flow_copy(s, xp):
        return remote(
            flow_out.at[s, pl.ds(pl.multiple_of(xp * part_rows, 16), part_rows)],
            flow_in.at[s, x],
            flow_sent.at[s, xp],
            flow_landed.at[s, x],
            c - gaps[s],
            2 * xp + kind,
        )

    def flow_wait(s, xs):
        remote(
            flow_out.at[s, pl.ds(0, part_rows)],
            flow_in.at[s, xs],
            flow_sent.at[s, 0],
            flow_landed.at[s, xs],
            c,
            sibling,
        ).wait_recv()

    others = [lax.rem(x + o, parts) for o in range(1, parts)]

    def pass_on(s):
        swap_copy(s).wait_recv()
        joined = keep[s] + swap_in[s].astype(F32)
        if s == 0:
            keep[0] = joined
        flow_out[s] = joined.astype(LOW)
        for xp in range(parts) if s else others:
            flow_copy(s, xp).start()

    for s in range(sections - 1, 0, -1):
        pl.when(takes(s))(lambda: backward(s))
        if s + 1 < sections:
            pl.when(takes(s + 1))(lambda: pass_on(s + 1))
    backward(0)
    if sections > 1:
        pl.when(takes(1))(lambda: pass_on(1))
    pass_on(0)

    dq_buf[...] = dot(f[0], kv[0, 0], 1, 0) * top[0]
    for s in range(1, sections):

        @pl.when(takes(s))
        def _():
            dq_buf[...] += dot(f[s], kv[s, 0], 1, 0) * top[s]

    o_store.wait()
    low_buf[...] = (dq_buf[...] * scale).astype(LOW)
    dq_store = pltpu.make_async_copy(low_buf, dq_out, store_sem.at[1])
    dq_store.start()

    mine = pl.ds(pl.multiple_of(x * part_rows, 16), part_rows)
    total[...] = keep[0, mine]
    for xs in others:
        flow_wait(0, xs)
        total[...] += flow_in[0, xs].astype(F32)
    for s in range(1, sections):

        @pl.when(sends(s))
        def _():
            for xs in range(parts):
                flow_wait(s, xs)
                total[...] += flow_in[s, xs].astype(F32)

    final[...] = total[...].astype(LOW)

    def fin_copy(out, o):
        return remote(
            final, out.at[mine], fin_sent.at[o], fin_landed.at[o], c, lax.rem(h + o, head_width)
        )

    for which, out in ((0, dk_out), (1, dv_out)):

        @pl.when(kind == which)
        def _():
            for o in range(1, head_width):
                fin_copy(out, o).start()
            own = pltpu.make_async_copy(final, out.at[mine], store_sem.at[2])
            own.start()
            own.wait()

    for o in range(1, head_width):
        source = lax.rem(h + head_width - o, head_width)
        there = pl.ds(pl.multiple_of(lax.div(source, 2) * part_rows, 16), part_rows)
        for which, out in ((0, dk_out), (1, dv_out)):

            @pl.when(lax.rem(source, 2) == which)
            def _():
                remote(
                    final, out.at[there], fin_sent.at[o], fin_landed.at[o], c, source
                ).wait_recv()

    for s in range(1, sections):
        pl.when(sends(s))(lambda: kv_copy(s).wait_send())

        @pl.when(takes(s))
        def _():
            pair_copy(s, kind).wait_send()
            swap_copy(s).wait_send()
            for xp in range(parts):
                flow_copy(s, xp).wait_send()

    swap_copy(0).wait_send()
    for xp in others:
        flow_copy(0, xp).wait_send()
    for o in range(1, head_width):
        fin_copy(dk_out, o).wait_send()
    dq_store.wait()


def write_out(*refs):
    sources, targets, sem = refs[:4], refs[4:8], refs[8]
    copies = [
        pltpu.make_async_copy(source, target, sem.at[i])
        for i, (source, target) in enumerate(zip(sources, targets))
    ]
    for copy in copies:
        copy.start()
    for copy in copies:
        copy.wait()


def local(ctx_width, head_width, queries, key_rows, value_rows, grad_out, doc_lengths, block_pattern):
    tok_rows, group, dim = queries.shape
    rows = tok_rows * group
    sections = ctx_width.bit_length()
    parts = head_width // 2
    part_rows = tok_rows // parts
    anywhere = pl.BlockSpec(memory_space=pl.ANY)
    dma = pltpu.SemaphoreType.DMA
    outs = pl.pallas_call(
        functools.partial(kernel, ctx_width, head_width, group),
        out_shape=(
            jax.ShapeDtypeStruct((rows, dim), LOW),
            jax.ShapeDtypeStruct((rows, dim), LOW),
            jax.ShapeDtypeStruct((tok_rows, dim), LOW),
            jax.ShapeDtypeStruct((tok_rows, dim), LOW),
        ),
        in_specs=[
            anywhere,
        ]
        * 6,
        out_specs=(anywhere,) * 4,
        scratch_shapes=[
            pltpu.VMEM((sections, 2, tok_rows, dim), LOW),
            pltpu.VMEM((rows, dim), LOW),
            pltpu.VMEM((rows, dim), LOW),
            pltpu.VMEM((sections, rows, tok_rows), LOW),
            pltpu.VMEM((sections, rows, tok_rows), LOW),
            pltpu.VMEM((sections, rows, tok_rows), F32),
            pltpu.VMEM((sections, rows, dim), F32),
            pltpu.VMEM((sections, rows, dim), F32),
            pltpu.VMEM((sections, rows, dim), F32),
            pltpu.VMEM((rows, dim), F32),
            pltpu.VMEM((rows, dim), LOW),
            pltpu.VMEM((rows, dim), F32),
            pltpu.VMEM((sections, tok_rows, dim), F32),
            pltpu.VMEM((sections, tok_rows, dim), LOW),
            pltpu.VMEM((sections, tok_rows, dim), LOW),
            pltpu.VMEM((sections, tok_rows, dim), LOW),
            pltpu.VMEM((sections, parts, part_rows, dim), LOW),
            pltpu.VMEM((part_rows, dim), F32),
            pltpu.VMEM((part_rows, dim), LOW),
            pltpu.SMEM(block_pattern.shape, jnp.int32),
            pltpu.VMEM((1, doc_lengths.shape[0]), jnp.int32),
            dma((6,)),
            dma((3,)),
            dma((sections,)),
            dma((sections,)),
            dma((sections,)),
            dma((sections,)),
            dma((sections,)),
            dma((sections,)),
            dma((sections, parts)),
            dma((sections, parts)),
            dma((head_width,)),
            dma((head_width,)),
        ],
        compiler_params=pltpu.CompilerParams(
            collective_id=0,
            has_side_effects=True,
            vmem_limit_bytes=60 * 1024 * 1024,
        ),
    )(
        block_pattern,
        doc_lengths.reshape(1, -1),
        queries.reshape(rows, dim),
        key_rows,
        value_rows,
        grad_out.reshape(rows, dim),
    )
    outs = pl.pallas_call(
        write_out,
        out_shape=tuple(jax.ShapeDtypeStruct(out.shape, out.dtype) for out in outs),
        in_specs=[pl.BlockSpec(memory_space=pltpu.VMEM)] * 4,
        out_specs=(anywhere,) * 4,
        scratch_shapes=[dma((4,))],
    )(*outs)
    attn_out, grad_queries, grad_keys, grad_values = outs
    shape = (tok_rows, group, dim)
    return (attn_out.reshape(shape), grad_queries.reshape(shape), grad_keys, grad_values)


def solution(mesh):
    placed = (
        P("ctx", "head", None),
        P("ctx", None),
        P("ctx", None),
        P("ctx", "head", None),
        P(),
        P("ctx", None),
    )
    return jax.shard_map(
        functools.partial(local, mesh.shape["ctx"], mesh.shape["head"]),
        mesh=mesh,
        in_specs=placed,
        out_specs=(P("ctx", "head", None), P("ctx", "head", None), P("ctx", None), P("ctx", None)),
        check_vma=False,
    )
```

```python
import functools
import math

import jax
import jax.numpy as jnp
from jax import lax
from jax.experimental import pallas as pl
from jax.experimental.pallas import tpu as pltpu
from jax.sharding import PartitionSpec as P

NEG_FILL = -1e30
FAR = 1e9
MESH = pl.DeviceIdType.MESH
F32 = jnp.float32
LOW = jnp.bfloat16


def dot(a, b, dim_a, dim_b):
    return lax.dot_general(
        a, b, (((dim_a,), (dim_b,)), ((), ())), preferred_element_type=F32
    )


def remote(src, dst, sent, landed, ctx, head):
    return pltpu.make_async_remote_copy(
        src_ref=src,
        dst_ref=dst,
        send_sem=sent,
        recv_sem=landed,
        device_id=(ctx, head),
        device_id_type=MESH,
    )


def kernel(
    ctx_width, head_width, group, pattern_in, lengths_in, q_in, k_in, v_in, g_in,
    o_out, dq_out, dk_out, dv_out,
    kv, q, g, e, f, dp, top, tot, acc, mean, low_buf, dq_buf,
    keep, swap_out, swap_in, flow_out, flow_in, total, final, pattern, lengths,
    load_sem, store_sem, kv_sent, kv_landed, pair_sent, pair_landed,
    swap_sent, swap_landed, flow_sent, flow_landed, fin_sent, fin_landed,
):
    tok_rows, dim = k_in.shape
    rows = q_in.shape[0]
    block_count = pattern.shape[0]
    block = tok_rows // block_count
    block_q = block * group
    sections = kv.shape[0]
    parts = head_width // 2
    part_rows = tok_rows // parts
    scale = 1.0 / math.sqrt(dim)
    first_doc = 3 * ctx_width // 4
    c = lax.axis_index("ctx")
    h = lax.axis_index("head")
    kind = lax.rem(h, 2)
    x = lax.div(h, 2)
    sibling = h + 1 - 2 * kind
    gaps = [0] + [1 << bit for bit in range(sections - 1)]

    def sends(s):
        d = gaps[s]
        crosses = jnp.logical_and(c < first_doc, c + d >= first_doc)
        return jnp.logical_and(c + d < ctx_width, jnp.logical_not(crosses))

    def takes(s):
        d = gaps[s]
        crosses = jnp.logical_and(c - d < first_doc, c >= first_doc)
        return jnp.logical_and(c - d >= 0, jnp.logical_not(crosses))

    loads = [
        pltpu.make_async_copy(k_in, kv.at[0, 0], load_sem.at[0]),
        pltpu.make_async_copy(v_in, kv.at[0, 1], load_sem.at[1]),
        pltpu.make_async_copy(q_in, q, load_sem.at[2]),
        pltpu.make_async_copy(g_in, g, load_sem.at[3]),
        pltpu.make_async_copy(pattern_in, pattern, load_sem.at[4]),
        pltpu.make_async_copy(lengths_in, lengths, load_sem.at[5]),
    ]
    for load in loads:
        load.start()

    barrier = pltpu.get_barrier_semaphore()
    expected = jnp.int32(head_width - 1)
    for o in range(1, head_width):
        pl.semaphore_signal(
            barrier, inc=1, device_id=(c, lax.rem(h + o, head_width)), device_id_type=MESH
        )
    for s in range(1, sections):
        for sign, active in ((1, sends(s)), (-1, takes(s))):
            expected = expected + jnp.where(active, parts, 0)

            @pl.when(active)
            def _():
                for xp in range(parts):
                    pl.semaphore_signal(
                        barrier,
                        inc=1,
                        device_id=(c + sign * gaps[s], 2 * xp + kind),
                        device_id_type=MESH,
                    )
    pl.semaphore_wait(barrier, expected)

    def kv_copy(s):
        return remote(
            kv.at[0, kind], kv.at[s, kind], kv_sent.at[s], kv_landed.at[s], c + gaps[s], h
        )

    def pair_copy(s, which):
        return remote(
            kv.at[s, which], kv.at[s, which], pair_sent.at[s], pair_landed.at[s], c, sibling
        )

    loads[0].wait()
    loads[1].wait()
    for s in range(1, sections):
        pl.when(sends(s))(lambda: kv_copy(s).start())
    for load in loads[2:]:
        load.wait()

    doc_count = lengths.shape[1]
    len_row = lengths[...].astype(F32)
    row_id = lax.broadcasted_iota(jnp.int32, (doc_count, doc_count), 0)
    col_id = lax.broadcasted_iota(jnp.int32, (doc_count, doc_count), 1)
    len_col = jnp.sum(jnp.where(row_id == col_id, len_row, 0.0), axis=1, keepdims=True)
    ends = jnp.sum(jnp.where(row_id <= col_id, len_col, 0.0), axis=0, keepdims=True)
    shift = group.bit_length() - 1
    local_pos = lax.shift_right_logical(
        lax.broadcasted_iota(jnp.int32, (rows, doc_count), 0), shift
    )
    pos = (local_pos + c * tok_rows).astype(F32)
    begin = jnp.max(jnp.where(ends <= pos, ends, 0.0), axis=1, keepdims=True)
    lane = lax.broadcasted_iota(jnp.int32, (block_q, block), 1).astype(F32)
    in_block = lax.shift_right_logical(
        lax.broadcasted_iota(jnp.int32, (block_q, block), 0), shift
    ).astype(F32)
    log_scale = scale * math.log2(math.e)

    def forward(s):
        p = c - gaps[s]
        keys = kv[s, 0]
        values = kv[s, 1]
        with_ones = jnp.concatenate([values, jnp.ones((tok_rows, dim), LOW)], axis=1)
        for i in range(block_count):
            at = pl.ds(i * block_q, block_q)
            raw = dot(q[at], keys, 1, 1)
            tiles = []
            for j in range(block_count):
                tile = raw[:, j * block : (j + 1) * block] * log_scale
                if s == 0 and j > i:
                    tiles.append(jnp.full_like(tile, NEG_FILL))
                    continue
                base = (p * tok_rows + j * block).astype(F32)
                least = begin[i * block_q : (i + 1) * block_q] - base
                least = jnp.where(pattern[i, p * block_count + j] == 1, least, FAR)
                live = lane >= least
                if s == 0 and j == i:
                    live = jnp.logical_and(live, lane <= in_block)
                tiles.append(jnp.where(live, tile, NEG_FILL))
            scores = jnp.concatenate(tiles, axis=1)
            high = jnp.max(scores, axis=1, keepdims=True)
            ex = jnp.exp2(scores - high).astype(LOW)
            e[s, at] = ex
            top[s, at] = jnp.broadcast_to(high, (block_q, dim))
            both = dot(ex, with_ones, 1, 0)
            acc[s, at] = both[:, :dim]
            tot[s, at] = both[:, dim:]
            dp[s, at] = dot(g[at], values, 1, 1)

    forward(0)

    def relay(s):
        @pl.when(takes(s))
        def _():
            kv_copy(s).wait_recv()
            pair_copy(s, kind).start()

    if sections > 1:
        relay(1)
    for s in range(1, sections):
        if s + 1 < sections:
            relay(s + 1)
        active = takes(s)

        @pl.when(active)
        def _():
            pair_copy(s, 1 - kind).wait_recv()
            forward(s)

        @pl.when(jnp.logical_not(active))
        def _():
            top[s] = jnp.full((rows, dim), NEG_FILL, F32)
            tot[s] = jnp.zeros((rows, dim), F32)
            acc[s] = jnp.zeros((rows, dim), F32)

    for i in range(block_count):
        at = pl.ds(i * block_q, block_q)
        high = top[0, at]
        for s in range(1, sections):
            high = jnp.maximum(high, top[s, at])
        row_total = jnp.zeros((block_q, dim), F32)
        out = jnp.zeros((block_q, dim), F32)
        weights = []
        for s in range(sections):
            w = jnp.exp2(top[s, at] - high)
            weights.append(w)
            row_total = row_total + w * tot[s, at]
            out = out + w * acc[s, at]
        inverse = 1.0 / row_total
        low = (out * inverse).astype(LOW)
        low_buf[at] = low
        for s in range(sections):
            top[s, at] = weights[s] * inverse
        dots = jnp.sum(g[at].astype(F32) * low.astype(F32), axis=1, keepdims=True)
        mean[at] = jnp.broadcast_to(dots, (block_q, dim))
    o_store = pltpu.make_async_copy(low_buf, o_out, store_sem.at[0])
    o_store.start()

    def swap_copy(s):
        return remote(
            swap_out.at[s], swap_in.at[s], swap_sent.at[s], swap_landed.at[s], c, sibling
        )

    def backward(s):
        for i in range(block_count):
            at = pl.ds(i * block_q, block_q)
            centre = mean[at]
            for j in range(block_count):
                lanes = pl.ds(j * block, block)
                f[s, at, lanes] = (
                    e[s, at, lanes].astype(F32) * (dp[s, at, lanes] - centre)
                ).astype(LOW)
        ratio = top[s]
        q_scaled = (q[...].astype(F32) * (ratio * scale)).astype(LOW)
        g_scaled = (g[...].astype(F32) * ratio).astype(LOW)
        dk = dot(f[s], q_scaled, 0, 0)
        dv = dot(e[s], g_scaled, 0, 0)
        keep[s] = jnp.where(kind == 0, dk, dv)
        swap_out[s] = jnp.where(kind == 0, dv, dk).astype(LOW)
        swap_copy(s).start()

    def flow_copy(s, xp):
        return remote(
            flow_out.at[s, pl.ds(pl.multiple_of(xp * part_rows, 16), part_rows)],
            flow_in.at[s, x],
            flow_sent.at[s, xp],
            flow_landed.at[s, x],
            c - gaps[s],
            2 * xp + kind,
        )

    def flow_wait(s, xs):
        remote(
            flow_out.at[s, pl.ds(0, part_rows)],
            flow_in.at[s, xs],
            flow_sent.at[s, 0],
            flow_landed.at[s, xs],
            c,
            sibling,
        ).wait_recv()

    others = [lax.rem(x + o, parts) for o in range(1, parts)]

    def pass_on(s):
        swap_copy(s).wait_recv()
        joined = keep[s] + swap_in[s].astype(F32)
        if s == 0:
            keep[0] = joined
        flow_out[s] = joined.astype(LOW)
        for xp in others + [x] if s else others:
            flow_copy(s, xp).start()

    for s in range(sections - 1, 0, -1):
        pl.when(takes(s))(lambda: backward(s))
        if s + 1 < sections:
            pl.when(takes(s + 1))(lambda: pass_on(s + 1))
    backward(0)
    if sections > 1:
        pl.when(takes(1))(lambda: pass_on(1))
    pass_on(0)

    dq_buf[...] = dot(f[0], kv[0, 0], 1, 0) * top[0]
    for s in range(1, sections):

        @pl.when(takes(s))
        def _():
            dq_buf[...] += dot(f[s], kv[s, 0], 1, 0) * top[s]

    o_store.wait()
    low_buf[...] = (dq_buf[...] * scale).astype(LOW)
    dq_store = pltpu.make_async_copy(low_buf, dq_out, store_sem.at[1])
    dq_store.start()

    mine = pl.ds(pl.multiple_of(x * part_rows, 16), part_rows)
    total[...] = keep[0, mine]
    for xs in others:
        flow_wait(0, xs)
        total[...] += flow_in[0, xs].astype(F32)
    for s in range(1, sections):

        @pl.when(sends(s))
        def _():
            for xs in range(parts):
                flow_wait(s, xs)
                total[...] += flow_in[s, xs].astype(F32)

    final[...] = total[...].astype(LOW)

    def fin_copy(out, o):
        return remote(
            final, out.at[mine], fin_sent.at[o], fin_landed.at[o], c, lax.rem(h + o, head_width)
        )

    for which, out in ((0, dk_out), (1, dv_out)):

        @pl.when(kind == which)
        def _():
            for o in range(1, head_width):
                fin_copy(out, o).start()
            own = pltpu.make_async_copy(final, out.at[mine], store_sem.at[2])
            own.start()
            own.wait()

    for o in range(1, head_width):
        source = lax.rem(h + head_width - o, head_width)
        there = pl.ds(pl.multiple_of(lax.div(source, 2) * part_rows, 16), part_rows)
        for which, out in ((0, dk_out), (1, dv_out)):

            @pl.when(lax.rem(source, 2) == which)
            def _():
                remote(
                    final, out.at[there], fin_sent.at[o], fin_landed.at[o], c, source
                ).wait_recv()

    for s in range(1, sections):
        pl.when(sends(s))(lambda: kv_copy(s).wait_send())

        @pl.when(takes(s))
        def _():
            pair_copy(s, kind).wait_send()
            swap_copy(s).wait_send()
            for xp in range(parts):
                flow_copy(s, xp).wait_send()

    swap_copy(0).wait_send()
    for xp in others:
        flow_copy(0, xp).wait_send()
    for o in range(1, head_width):
        fin_copy(dk_out, o).wait_send()
    dq_store.wait()


def write_out(*refs):
    sources, targets, sem = refs[:4], refs[4:8], refs[8]
    copies = [
        pltpu.make_async_copy(source, target, sem.at[i])
        for i, (source, target) in enumerate(zip(sources, targets))
    ]
    for copy in copies:
        copy.start()
    for copy in copies:
        copy.wait()


def local(ctx_width, head_width, queries, key_rows, value_rows, grad_out, doc_lengths, block_pattern):
    tok_rows, group, dim = queries.shape
    rows = tok_rows * group
    sections = ctx_width.bit_length()
    parts = head_width // 2
    part_rows = tok_rows // parts
    anywhere = pl.BlockSpec(memory_space=pl.ANY)
    dma = pltpu.SemaphoreType.DMA
    outs = pl.pallas_call(
        functools.partial(kernel, ctx_width, head_width, group),
        out_shape=(
            jax.ShapeDtypeStruct((rows, dim), LOW),
            jax.ShapeDtypeStruct((rows, dim), LOW),
            jax.ShapeDtypeStruct((tok_rows, dim), LOW),
            jax.ShapeDtypeStruct((tok_rows, dim), LOW),
        ),
        in_specs=[
            anywhere,
        ]
        * 6,
        out_specs=(anywhere,) * 4,
        scratch_shapes=[
            pltpu.VMEM((sections, 2, tok_rows, dim), LOW),
            pltpu.VMEM((rows, dim), LOW),
            pltpu.VMEM((rows, dim), LOW),
            pltpu.VMEM((sections, rows, tok_rows), LOW),
            pltpu.VMEM((sections, rows, tok_rows), LOW),
            pltpu.VMEM((sections, rows, tok_rows), F32),
            pltpu.VMEM((sections, rows, dim), F32),
            pltpu.VMEM((sections, rows, dim), F32),
            pltpu.VMEM((sections, rows, dim), F32),
            pltpu.VMEM((rows, dim), F32),
            pltpu.VMEM((rows, dim), LOW),
            pltpu.VMEM((rows, dim), F32),
            pltpu.VMEM((sections, tok_rows, dim), F32),
            pltpu.VMEM((sections, tok_rows, dim), LOW),
            pltpu.VMEM((sections, tok_rows, dim), LOW),
            pltpu.VMEM((sections, tok_rows, dim), LOW),
            pltpu.VMEM((sections, parts, part_rows, dim), LOW),
            pltpu.VMEM((part_rows, dim), F32),
            pltpu.VMEM((part_rows, dim), LOW),
            pltpu.SMEM(block_pattern.shape, jnp.int32),
            pltpu.VMEM((1, doc_lengths.shape[0]), jnp.int32),
            dma((6,)),
            dma((3,)),
            dma((sections,)),
            dma((sections,)),
            dma((sections,)),
            dma((sections,)),
            dma((sections,)),
            dma((sections,)),
            dma((sections, parts)),
            dma((sections, parts)),
            dma((head_width,)),
            dma((head_width,)),
        ],
        compiler_params=pltpu.CompilerParams(
            collective_id=0,
            has_side_effects=True,
            vmem_limit_bytes=60 * 1024 * 1024,
        ),
    )(
        block_pattern,
        doc_lengths.reshape(1, -1),
        queries.reshape(rows, dim),
        key_rows,
        value_rows,
        grad_out.reshape(rows, dim),
    )
    outs = pl.pallas_call(
        write_out,
        out_shape=tuple(jax.ShapeDtypeStruct(out.shape, out.dtype) for out in outs),
        in_specs=[pl.BlockSpec(memory_space=pltpu.VMEM)] * 4,
        out_specs=(anywhere,) * 4,
        scratch_shapes=[dma((4,))],
    )(*outs)
    attn_out, grad_queries, grad_keys, grad_values = outs
    shape = (tok_rows, group, dim)
    return (attn_out.reshape(shape), grad_queries.reshape(shape), grad_keys, grad_values)


def solution(mesh):
    placed = (
        P("ctx", "head", None),
        P("ctx", None),
        P("ctx", None),
        P("ctx", "head", None),
        P(),
        P("ctx", None),
    )
    return jax.shard_map(
        functools.partial(local, mesh.shape["ctx"], mesh.shape["head"]),
        mesh=mesh,
        in_specs=placed,
        out_specs=(P("ctx", "head", None), P("ctx", "head", None), P("ctx", None), P("ctx", None)),
        check_vma=False,
    )
```
